32 devices in a mesh: blk: 8 (over z, y), tp: 4 (over x, core).
Axes of the slice: x: 2, y: 2, z: 4, core: 2. Of those that a mesh axis runs over, the one named last changes fastest.
Arguments:
- tokens: bfloat16 [4096, 1664], P('blk', 'tp'), may hold values from -8 to 8
- block_split: int32 [16], replicated, may hold values from 0 to 15, each once
- req_lengths: int32 [32], replicated, may hold values from 1 to 125, as said below
- req_owners: int32 [32], replicated, may hold values from 0 to 7, as said below
- norm1_gain: float32 [1664], replicated, may hold values from 0.25 to 1.75
- qkv_weight: bfloat16 [1664, 3, 1664], P(None, None, 'tp'), may hold values from -2 to 2
- out_weight: bfloat16 [1664, 1664], P('tp'), may hold values from -0.15625 to 0.15625
- norm2_gain: float32 [1664], replicated, may hold values from 0.25 to 1.75
- up_weight: bfloat16 [1664, 8192], P(None, 'tp'), may hold values from -0.15625 to 0.15625
- down_weight: bfloat16 [8192, 1664], P('tp'), may hold values from -0.0625 to 0.0625
- merge_gain: float32 [1664], replicated, may hold values from 0.25 to 1.75
- merge_weight: bfloat16 [6656, 1664], P(None, 'tp'), may hold values from -0.078125 to 0.078125
Outputs:
- returned: bfloat16 [1024, 1664], P('blk', 'tp')
The draws below stay inside these ranges and needn't reach their ends.
Inputs may be any that keep to these rules, and one draw needn't show every extreme that they name: Index d of blk holds packed blocks block_split[2d] and block_split[2d + 1], each of 256 tokens; every block once. `req_lengths`: lengths count merge groups of 4 tokens; the requests of each owner add up to exactly 128 groups. `req_owners`: every owner index holds exactly 4 requests.
All inputs are finite; a program needn't handle non-finite values.
Results may differ from the reference program's by a relative error of at most 0.015.
Values may be sent and summed in bfloat16 or wider, within the bound.
A program may use at most 128 MiB of HBM per device.

```python
import jax
import jax.numpy as jnp
from jax import lax

D = 1664
HEADS = 16
FF = 8192
HDIM = 104
TOK_DEV = 512
REQ_OWN = 4
GROUP_DEV = 128
TOKENS = 4096
NREQ = 32
MERGED = 1024
N_BLK = 8
N_TP = 4


def request_plan(key):
    plan_key = jax.random.fold_in(key, 11)
    owner_total = NREQ // REQ_OWN

    def one_owner(owner_index):
        owner_key = jax.random.fold_in(plan_key, owner_index)
        random_cuts = jax.random.permutation(owner_key, GROUP_DEV - 1)[:REQ_OWN - 1] + 1
        fixed_cuts = jnp.arange(1, REQ_OWN, dtype=jnp.int32)
        cut_points = jnp.where(owner_index == 0, fixed_cuts, random_cuts.astype(jnp.int32))
        cut_points = jnp.sort(cut_points.astype(jnp.int32))
        bounds = jnp.concatenate([jnp.zeros((1,), jnp.int32), cut_points, jnp.full((1,), GROUP_DEV, jnp.int32)])
        return bounds[1:] - bounds[:-1]
    owner_sizes = jax.vmap(one_owner)(jnp.arange(owner_total, dtype=jnp.int32))
    pack_order = jax.random.permutation(jax.random.fold_in(plan_key, 99991), NREQ)
    flat_sizes = owner_sizes.reshape(-1)[pack_order]
    flat_owners = (jnp.arange(NREQ, dtype=jnp.int32) // REQ_OWN)[pack_order]
    return (flat_sizes.astype(jnp.int32), flat_owners.astype(jnp.int32))


def draw_req_lengths(key, part):
    return request_plan(key)[0]


def draw_req_owners(key, part):
    return request_plan(key)[1]


def draw_tokens(key, part):
    normal_key = jax.random.fold_in(key, 0)
    sampled = jax.random.normal(normal_key, (TOKENS, D), jnp.float32)
    return jnp.clip(sampled, -8.0, 8.0).astype(jnp.bfloat16)


def draw_qkv_weight(key, part):
    sampled = jax.random.normal(key, (D, 3, D), jnp.float32) * D ** (-0.5)
    return jnp.clip(sampled, -2.0, 2.0).astype(jnp.bfloat16)


def block_levels(stream_key, shape, shards, low, high):
    level, own = 1.0, jax.random.fold_in(stream_key, 6)
    for dim, shards_of in shards:
        steps = jnp.exp(jax.random.uniform(jax.random.fold_in(own, dim), (shards_of,), jnp.float32, low / len(shards), high / len(shards)))
        level = level * jnp.repeat(steps, shape[dim] // shards_of).reshape([-1 if axis == dim else 1 for axis in range(len(shape))])
    return level


def scatter_about(own_key, shape, scale, limit, shards=(), kind=jnp.bfloat16):
    values = scale * jax.random.normal(own_key, shape, jnp.float32)
    if shards:
        values = values * block_levels(own_key, shape, shards, -0.22, 0.18)
    return jnp.clip(values, -limit, limit).astype(kind)


def setup_inputs(seed: int = 0) -> dict:
    key_list = jax.random.split(jax.random.key(seed), 13)
    return {
        "tokens": draw_tokens(jax.random.fold_in(key_list[12], 71), 0),
        "block_split": jax.random.permutation(key_list[1], 2 * N_BLK).astype(jnp.int32),
        "req_lengths": draw_req_lengths(jax.random.fold_in(key_list[12], 71), 0),
        "req_owners": draw_req_owners(jax.random.fold_in(key_list[12], 71), 0),
        "norm1_gain": jnp.clip(1.0 + 0.15 * jax.random.normal(key_list[4], (D,), jnp.float32), 0.25, 1.75),
        "qkv_weight": draw_qkv_weight(jax.random.fold_in(key_list[12], 71), 0),
        "out_weight": scatter_about(key_list[6], (D, D), D ** -0.5, 0.15625, ((0, 4),)),
        "norm2_gain": jnp.clip(1.0 + 0.15 * jax.random.normal(key_list[7], (D,), jnp.float32), 0.25, 1.75),
        "up_weight": scatter_about(key_list[8], (D, FF), D ** -0.5, 0.15625, ((1, 4),)),
        "down_weight": scatter_about(key_list[9], (FF, D), FF ** -0.5, 0.0625, ((0, 4),)),
        "merge_gain": jnp.clip(1.0 + 0.15 * jax.random.normal(key_list[10], (D,), jnp.float32), 0.25, 1.75),
        "merge_weight": scatter_about(key_list[11], (4 * D, D), (4 * D) ** -0.5, 0.078125, ((1, 4),)),
    }


EPSILON = 1e-06
MASKED = -1e+30

def layer_norm(values, norm_gain):
    values = values.astype(jnp.float32)
    row_mean = lax.optimization_barrier(jnp.mean(values, axis=-1, keepdims=True))
    centred = values - row_mean
    spread = lax.optimization_barrier(jnp.mean(centred * centred, axis=-1, keepdims=True))
    return centred * lax.rsqrt(spread + EPSILON) * norm_gain

def request_tables(req_lengths, req_owners):
    request_ends = jnp.cumsum(req_lengths).astype(jnp.int32)
    starts = request_ends - req_lengths
    position = jnp.arange(req_lengths.shape[0], dtype=jnp.int32)
    earlier = (req_owners[None, :] == req_owners[:, None]) & (position[None, :] < position[:, None])
    owner_offset = lax.optimization_barrier(jnp.sum(jnp.where(earlier, req_lengths[None, :], 0), axis=1)).astype(jnp.int32)
    return (starts, request_ends, owner_offset)

def attend(carried, query_rows, query_seg, key_rows, value_rows, key_seg):
    maxima, totals, accumulated = carried
    query_count = query_rows.shape[0]
    key_count = key_rows.shape[0]
    head_count = accumulated.shape[1]
    head_size = accumulated.shape[2]
    query_heads = query_rows.reshape(query_count, head_count, head_size).astype(jnp.float32)
    key_heads = key_rows.reshape(key_count, head_count, head_size).astype(jnp.float32)
    value_heads = value_rows.reshape(key_count, head_count, head_size).astype(jnp.float32)
    scores = jnp.einsum('qhd,khd->hqk', query_heads, key_heads) * head_size ** (-0.5)
    same_request = (query_seg[:, None] == key_seg[None, :])[None, :, :]
    scores = jnp.where(same_request, scores, MASKED)
    new_max = jnp.maximum(maxima, lax.optimization_barrier(jnp.max(scores, axis=2)))
    weights = jnp.where(same_request, jnp.exp(scores - new_max[:, :, None]), 0.0)
    factor = jnp.exp(maxima - new_max)
    totals = totals * factor + lax.optimization_barrier(jnp.sum(weights, axis=2))
    mixed_values = jnp.einsum('hqk,khd->qhd', weights.astype(jnp.bfloat16).astype(jnp.float32), value_heads)
    accumulated = accumulated * jnp.transpose(factor)[:, :, None] + mixed_values
    return (new_max, totals, accumulated)

def split_sum(left, right, groups):
    group_width = left.shape[1] // groups
    total_sum = jnp.zeros((left.shape[0], right.shape[1]), jnp.float32)
    for group_index in range(groups):
        term = jnp.dot(left[:, group_index * group_width:(group_index + 1) * group_width], right[group_index * group_width:(group_index + 1) * group_width], preferred_element_type=jnp.float32)
        rounded = lax.optimization_barrier(term.astype(jnp.bfloat16))
        total_sum = total_sum + rounded.astype(jnp.float32)
    return total_sum

def reference(tokens, block_split, req_lengths, req_owners, norm1_gain, qkv_weight, out_weight, norm2_gain, up_weight, down_weight, merge_gain, merge_weight):
    half_rows = TOK_DEV // 2
    starts, request_ends, owner_offset = request_tables(req_lengths, req_owners)
    places = jnp.arange(2 * N_BLK, dtype=jnp.int32)
    packed_index = jnp.arange(TOKENS, dtype=jnp.int32)
    packed_block = packed_index // half_rows
    held_at = lax.optimization_barrier(jnp.sum(jnp.where(block_split[None, :] == packed_block[:, None], places[None, :], 0), axis=1)).astype(jnp.int32)
    packed = jnp.take(tokens, held_at * half_rows + packed_index % half_rows, axis=0)
    segment = lax.optimization_barrier(jnp.sum((request_ends[None, :] <= (packed_index // 4)[:, None]).astype(jnp.int32), axis=1)).astype(jnp.int32)
    normed1 = layer_norm(packed, norm1_gain).astype(jnp.bfloat16)
    projected = jnp.einsum('td,dcf->ctf', normed1.astype(jnp.float32), qkv_weight.astype(jnp.float32)).astype(jnp.bfloat16)
    pad_rows = jnp.zeros((TOK_DEV, D), jnp.bfloat16)
    key_pad = jnp.concatenate([pad_rows, projected[1], pad_rows], axis=0)
    value_pad = jnp.concatenate([pad_rows, projected[2], pad_rows], axis=0)
    seg_rim = jnp.full((TOK_DEV,), -1, jnp.int32)
    seg_pad = jnp.concatenate([seg_rim, segment, seg_rim], axis=0)
    queries = projected[0]

    def one_block(block_index):
        row_start = block_index * TOK_DEV
        query_rows = lax.dynamic_slice_in_dim(queries, row_start, TOK_DEV, 0)
        query_seg = lax.dynamic_slice_in_dim(segment, row_start, TOK_DEV, 0)
        key_rows = lax.dynamic_slice_in_dim(key_pad, row_start, 3 * TOK_DEV, 0)
        value_rows = lax.dynamic_slice_in_dim(value_pad, row_start, 3 * TOK_DEV, 0)
        key_seg = lax.dynamic_slice_in_dim(seg_pad, row_start, 3 * TOK_DEV, 0)
        start_state = (jnp.full((HEADS, TOK_DEV), MASKED, jnp.float32), jnp.zeros((HEADS, TOK_DEV), jnp.float32), jnp.zeros((TOK_DEV, HEADS, HDIM), jnp.float32))
        maxima, totals, accumulated = attend(start_state, query_rows, query_seg, key_rows, value_rows, key_seg)
        return (accumulated / jnp.transpose(totals)[:, :, None]).reshape(TOK_DEV, D).astype(jnp.bfloat16)
    attended = lax.map(one_block, jnp.arange(N_BLK, dtype=jnp.int32)).reshape(TOKENS, D)
    after_attention = packed.astype(jnp.float32) + split_sum(attended, out_weight, N_TP)
    normed2 = layer_norm(after_attention, norm2_gain).astype(jnp.bfloat16)
    hidden = jax.nn.gelu(jnp.dot(normed2, up_weight, preferred_element_type=jnp.float32), approximate=False).astype(jnp.bfloat16)
    after_mlp = after_attention + split_sum(hidden, down_weight, N_TP)
    final_norm = layer_norm(after_mlp, merge_gain).astype(jnp.bfloat16)
    merged = jnp.dot(final_norm.reshape(MERGED, 4 * D), merge_weight, preferred_element_type=jnp.float32).astype(jnp.bfloat16)
    group_index = jnp.arange(MERGED, dtype=jnp.int32)
    request = lax.optimization_barrier(jnp.sum((request_ends[None, :] <= group_index[:, None]).astype(jnp.int32), axis=1)).astype(jnp.int32)
    chosen = request[:, None] == jnp.arange(NREQ, dtype=jnp.int32)[None, :]
    target = lax.optimization_barrier(jnp.sum(jnp.where(chosen, (req_owners * GROUP_DEV + owner_offset - starts)[None, :], 0), axis=1)).astype(jnp.int32) + group_index
    return jnp.zeros_like(merged).at[target].set(merged)
```

```python
import jax
import jax.numpy as jnp
from jax import lax
from jax.experimental import pallas as pl
from jax.experimental.pallas import tpu as pltpu
from jax.sharding import PartitionSpec as P

HDIM = 104
EPSILON = 1e-06
MASKED = -1e30
PIECES = 4
TP = 4
MESH = pl.DeviceIdType.MESH


def norm_rows(values, norm_gain):
    row_mean = jnp.mean(values, axis=-1, keepdims=True)
    centred = values - row_mean
    spread = jnp.mean(centred * centred, axis=-1, keepdims=True)
    return centred * lax.rsqrt(spread + EPSILON) * norm_gain


def partners():
    me = lax.axis_index("tp")
    core = lax.rem(me, 2)
    side = me // 2
    near = side * 2 + (1 - core)
    far = (1 - side) * 2 + core
    across = (1 - side) * 2 + (1 - core)
    return me, near, far, across


def greet(near, far):
    barrier = pltpu.get_barrier_semaphore()
    for other in (near, far):
        pl.semaphore_signal(barrier, inc=1, device_id={"tp": other}, device_id_type=MESH)
    pl.semaphore_wait(barrier, 2)


def send(source, target, sems, index, other):
    return pltpu.make_async_remote_copy(
        src_ref=source,
        dst_ref=target,
        send_sem=sems.at[0, index],
        recv_sem=sems.at[1, index],
        device_id={"tp": other},
        device_id_type=MESH,
    )


def gather_kernel(x_ref, gain_ref, out_ref, rest_ref, held, far_sems, near_sems, pass_sems, own_sem):
    me, near, far, across = partners()
    rows = x_ref.shape[0]
    own_rows = rest_ref.shape[0]
    size = rows // PIECES
    own_copy = pltpu.make_async_copy(x_ref, held.at[me], own_sem)
    own_copy.start()
    greet(near, far)
    to_far, to_near, passed = [], [], []
    for i in range(PIECES):
        part = pl.ds(i * size, size)
        to_far.append(send(x_ref.at[part], held.at[me, part], far_sems, i, far))
        to_far[i].start()
    for i in range(PIECES):
        part = pl.ds(i * size, size)
        to_near.append(send(x_ref.at[part], held.at[me, part], near_sems, i, near))
        to_near[i].start()
    for i in range(PIECES):
        part = pl.ds(i * size, size)
        to_far[i].wait_recv()
        passed.append(send(held.at[far, part], held.at[far, part], pass_sems, i, near))
        passed[i].start()
    own_copy.wait()
    for i in range(PIECES):
        to_near[i].wait_recv()
        passed[i].wait_recv()
        for j in range(0, size, 64):
            part = pl.ds(i * size + j, 64)
            values = jnp.concatenate(
                [held[k, part].astype(jnp.float32) for k in range(TP)], axis=1
            )
            out_ref[part] = norm_rows(values, gain_ref[...]).astype(jnp.bfloat16)
    for j in range(0, own_rows, 64):
        part = pl.ds(pl.multiple_of(me * own_rows + j, 64), 64)
        rest_ref[pl.ds(j, 64)] = jnp.concatenate(
            [held[k, part].astype(jnp.float32) for k in range(TP)], axis=1
        )
    for i in range(PIECES):
        to_far[i].wait_send()
        to_near[i].wait_send()
        passed[i].wait_send()


def sum_kernel(
    part_ref, rest_ref, gain_ref, out_ref, after_ref,
    got_far, got_own, forward, got_side, sems,
):
    me, near, far, across = partners()
    own_rows = rest_ref.shape[0]
    size = own_rows // PIECES

    def rows(chunk, i):
        return pl.ds(pl.multiple_of(chunk * own_rows + i * size, size), size)

    greet(near, far)
    first, second, third, fourth, fifth, sixth = [], [], [], [], [], []
    for i in range(PIECES):
        here = pl.ds(i * size, size)
        first.append(send(part_ref.at[rows(across, i)], got_far.at[here], sems.at[0], i, near))
        first[i].start()
    for i in range(PIECES):
        here = pl.ds(i * size, size)
        second.append(send(part_ref.at[rows(near, i)], got_own.at[here], sems.at[1], i, near))
        second[i].start()
    for i in range(PIECES):
        here = pl.ds(i * size, size)
        first[i].wait_recv()
        forward[here] = (
            part_ref[rows(far, i)].astype(jnp.float32) + got_far[here].astype(jnp.float32)
        ).astype(jnp.bfloat16)
        third.append(send(forward.at[here], got_side.at[here], sems.at[2], i, far))
        third[i].start()
    for i in range(PIECES):
        here = pl.ds(i * size, size)
        second[i].wait_recv()
        third[i].wait_recv()
        total = rest_ref[here] + (
            part_ref[rows(me, i)].astype(jnp.float32)
            + got_own[here].astype(jnp.float32)
            + got_side[here].astype(jnp.float32)
        )
        after_ref[here] = total
        out_ref[rows(me, i)] = norm_rows(total, gain_ref[...]).astype(jnp.bfloat16)
        fourth.append(send(out_ref.at[rows(me, i)], out_ref.at[rows(me, i)], sems.at[3], i, far))
        fourth[i].start()
        fifth.append(send(out_ref.at[rows(me, i)], out_ref.at[rows(me, i)], sems.at[4], i, near))
        fifth[i].start()
    for i in range(PIECES):
        fourth[i].wait_recv()
        sixth.append(send(out_ref.at[rows(far, i)], out_ref.at[rows(far, i)], sems.at[5], i, near))
        sixth[i].start()
    for i in range(PIECES):
        fifth[i].wait_recv()
        sixth[i].wait_recv()
    for i in range(PIECES):
        for copies in (first, second, third, fourth, fifth, sixth):
            copies[i].wait_send()


def vmem(count):
    return [pl.BlockSpec(memory_space=pltpu.VMEM)] * count


def gather_norm(x, gain, collective_id):
    rows, width = x.shape
    full = width * TP
    pair = pltpu.SemaphoreType.DMA((2, PIECES))
    return pl.pallas_call(
        gather_kernel,
        out_shape=(
            jax.ShapeDtypeStruct((rows, full), jnp.bfloat16),
            jax.ShapeDtypeStruct((rows // TP, full), jnp.float32),
        ),
        in_specs=vmem(2),
        out_specs=tuple(vmem(2)),
        scratch_shapes=[
            pltpu.VMEM((TP, rows, width), jnp.bfloat16),
            pair, pair, pair, pltpu.SemaphoreType.DMA,
        ],
        compiler_params=pltpu.CompilerParams(
            collective_id=collective_id, has_side_effects=True, vmem_limit_bytes=40 * 2**20
        ),
        name="gather_norm",
    )(x, gain.reshape(1, -1))


def sum_norm(part, rest, gain, collective_id):
    rows, full = part.shape
    own = (rows // TP, full)
    return pl.pallas_call(
        sum_kernel,
        out_shape=(
            jax.ShapeDtypeStruct((rows, full), jnp.bfloat16),
            jax.ShapeDtypeStruct(own, jnp.float32),
        ),
        in_specs=vmem(3),
        out_specs=tuple(vmem(2)),
        scratch_shapes=[pltpu.VMEM(own, jnp.bfloat16)] * 4
        + [pltpu.SemaphoreType.DMA((6, 2, PIECES))],
        compiler_params=pltpu.CompilerParams(
            collective_id=collective_id, has_side_effects=True, vmem_limit_bytes=40 * 2**20
        ),
        name="sum_norm",
    )(part, rest, gain.reshape(1, -1))


def route(tokens, block_split, req_lengths, req_owners):
    count = lax.axis_size("blk")
    rows, width = tokens.shape
    groups = rows // 4
    block_groups = groups // 2
    each = groups // count
    requests = req_lengths.shape[0]
    room = (groups + (requests // count) * (count - 1)) // count
    room = (room + 3) // 4 * 4
    index = lax.axis_index("blk")
    position = jnp.arange(requests, dtype=jnp.int32)
    ends = jnp.sum(
        jnp.where(position[None, :] <= position[:, None], req_lengths[None, :], 0), axis=1
    )
    starts = ends - req_lengths
    earlier = (req_owners[None, :] == req_owners[:, None]) & (position[None, :] < position[:, None])
    offset = jnp.sum(jnp.where(earlier, req_lengths[None, :], 0), axis=1)
    spot = jnp.arange(groups, dtype=jnp.int32)
    local = (spot % each) * count + index
    place = (spot // each) * 2 + local // block_groups
    places = jnp.arange(block_split.shape[0], dtype=jnp.int32)
    block = jnp.sum(jnp.where(place[:, None] == places[None, :], block_split[None, :], 0), axis=1)
    packed = block * block_groups + local % block_groups
    inside = (starts[None, :] <= packed[:, None]) & (packed[:, None] < ends[None, :])
    goal = jnp.sum(
        jnp.where(inside, (req_owners * groups + offset - starts)[None, :], 0), axis=1
    ) + packed
    owner = goal // groups
    rank = jnp.sum(
        ((owner[None, :] == owner[:, None]) & (goal[None, :] < goal[:, None])).astype(jnp.int32),
        axis=1,
    )
    out_spot = owner * room + rank
    chosen = (
        (req_owners[None, :] == index)
        & (offset[None, :] <= spot[:, None])
        & (spot[:, None] < (offset + req_lengths)[None, :])
    )
    wanted = jnp.sum(jnp.where(chosen, (starts - offset)[None, :], 0), axis=1) + spot
    request = jnp.sum(jnp.where(chosen, position[None, :], 0), axis=1)
    via = wanted % count
    turn = jnp.sum(
        ((via[None, :] == via[:, None]) & (spot[None, :] < spot[:, None])).astype(jnp.int32), axis=1
    )
    in_spot = via * room + turn

    def pick(hot, array):
        return jnp.dot(
            hot.astype(jnp.bfloat16), array, preferred_element_type=jnp.float32
        ).astype(jnp.bfloat16)

    row = jnp.arange(rows, dtype=jnp.int32)
    via_row = row // (4 * each)
    q_row = row // 4 % each
    source = (q_row * count + via_row) * 4 + row % 4
    sent = pick(source[:, None] == row[None, :], tokens)
    held = lax.all_to_all(sent, "blk", 0, 0, tiled=True)
    row_goal = jnp.repeat(out_spot, 4) * 4 + row % 4
    slots = jnp.arange(count * room * 4, dtype=jnp.int32)
    sent = pick(slots[:, None] == row_goal[None, :], held)
    held = lax.all_to_all(sent, "blk", 0, 0, tiled=True)
    row_from = jnp.tile(in_spot, 4) * 4 + row // groups
    return pick(row_from[:, None] == slots[None, :], held), request


def body(
    tokens,
    block_split,
    req_lengths,
    req_owners,
    norm1_gain,
    qkv_weight,
    out_weight,
    norm2_gain,
    up_weight,
    down_weight,
    merge_gain,
    merge_weight,
):
    rows, width = tokens.shape
    groups = rows // 4
    routed, request = route(tokens, block_split, req_lengths, req_owners)
    normed1, rest = gather_norm(routed, norm1_gain, 1)
    projected = jnp.einsum(
        "td,dcf->ctf", normed1, qkv_weight, preferred_element_type=jnp.float32
    ).astype(jnp.bfloat16)
    heads = width // HDIM
    queries, keys, values = (projected[c].reshape(rows, heads, HDIM) for c in range(3))
    segment = jnp.tile(request, 4)
    same = (segment[:, None] == segment[None, :])[None, :, :]
    scores = jnp.einsum(
        "qhd,khd->hqk", queries, keys, preferred_element_type=jnp.float32
    ) * HDIM ** (-0.5)
    scores = jnp.where(same, scores, MASKED)
    weights = jnp.exp(scores - jnp.max(scores, axis=2, keepdims=True))
    totals = jnp.sum(weights, axis=2)
    mixed = jnp.einsum(
        "hqk,khd->qhd", weights.astype(jnp.bfloat16), values, preferred_element_type=jnp.float32
    )
    attended = (mixed / jnp.transpose(totals)[:, :, None]).reshape(rows, width).astype(jnp.bfloat16)
    part = jnp.dot(attended, out_weight, preferred_element_type=jnp.float32).astype(jnp.bfloat16)
    normed2, rest = sum_norm(part, rest, norm2_gain, 2)
    hidden = jax.nn.gelu(
        jnp.dot(normed2, up_weight, preferred_element_type=jnp.float32), approximate=False
    ).astype(jnp.bfloat16)
    part = jnp.dot(hidden, down_weight, preferred_element_type=jnp.float32).astype(jnp.bfloat16)
    final, unused = sum_norm(part, rest, merge_gain, 3)
    full = final.shape[1]
    merged = jnp.zeros((groups, merge_weight.shape[1]), jnp.float32)
    for k in range(4):
        merged = merged + jnp.dot(
            final[k * groups : (k + 1) * groups],
            merge_weight[k * full : (k + 1) * full],
            preferred_element_type=jnp.float32,
        )
    return merged.astype(jnp.bfloat16)


def solution(mesh):
    return jax.shard_map(
        body,
        mesh=mesh,
        in_specs=(
            P("blk", "tp"),
            P(),
            P(),
            P(),
            P(),
            P(None, None, "tp"),
            P("tp", None),
            P(),
            P(None, "tp"),
            P("tp", None),
            P(),
            P(None, "tp"),
        ),
        out_specs=P("blk", "tp"),
        check_vma=False,
    )
```

```python
import jax
import jax.numpy as jnp
from jax import lax
from jax.experimental import pallas as pl
from jax.experimental.pallas import tpu as pltpu
from jax.sharding import PartitionSpec as P

HDIM = 104
EPSILON = 1e-06
MASKED = -1e30
PIECES = 4
TP = 4
MESH = pl.DeviceIdType.MESH


def norm_rows(values, norm_gain):
    row_mean = jnp.mean(values, axis=-1, keepdims=True)
    centred = values - row_mean
    spread = jnp.mean(centred * centred, axis=-1, keepdims=True)
    return centred * lax.rsqrt(spread + EPSILON) * norm_gain


def partners():
    me = lax.axis_index("tp")
    core = lax.rem(me, 2)
    side = me // 2
    near = side * 2 + (1 - core)
    far = (1 - side) * 2 + core
    across = (1 - side) * 2 + (1 - core)
    return me, near, far, across


def greet(near, far):
    barrier = pltpu.get_barrier_semaphore()
    for other in (near, far):
        pl.semaphore_signal(barrier, inc=1, device_id={"tp": other}, device_id_type=MESH)
    pl.semaphore_wait(barrier, 2)


def send(source, target, sems, index, other):
    return pltpu.make_async_remote_copy(
        src_ref=source,
        dst_ref=target,
        send_sem=sems.at[0, index],
        recv_sem=sems.at[1, index],
        device_id={"tp": other},
        device_id_type=MESH,
    )


def gather_kernel(x_ref, gain_ref, out_ref, rest_ref, held, far_sems, near_sems, pass_sems, own_sem):
    me, near, far, across = partners()
    rows = x_ref.shape[0]
    own_rows = rest_ref.shape[0]
    size = rows // PIECES
    own_copy = pltpu.make_async_copy(x_ref, held.at[me], own_sem)
    own_copy.start()
    greet(near, far)
    to_far, to_near, passed = [], [], []
    for i in range(PIECES):
        part = pl.ds(i * size, size)
        to_far.append(send(x_ref.at[part], held.at[me, part], far_sems, i, far))
        to_far[i].start()
    for i in range(PIECES):
        part = pl.ds(i * size, size)
        to_near.append(send(x_ref.at[part], held.at[me, part], near_sems, i, near))
        to_near[i].start()
    for i in range(PIECES):
        part = pl.ds(i * size, size)
        to_far[i].wait_recv()
        passed.append(send(held.at[far, part], held.at[far, part], pass_sems, i, near))
        passed[i].start()
    own_copy.wait()
    for i in range(PIECES):
        to_near[i].wait_recv()
        passed[i].wait_recv()
        for j in range(0, size, 64):
            part = pl.ds(i * size + j, 64)
            values = jnp.concatenate(
                [held[k, part].astype(jnp.float32) for k in range(TP)], axis=1
            )
            out_ref[part] = norm_rows(values, gain_ref[...]).astype(jnp.bfloat16)
    for j in range(0, own_rows, 64):
        part = pl.ds(pl.multiple_of(me * own_rows + j, 64), 64)
        rest_ref[pl.ds(j, 64)] = jnp.concatenate(
            [held[k, part].astype(jnp.float32) for k in range(TP)], axis=1
        )
    for i in range(PIECES):
        to_far[i].wait_send()
        to_near[i].wait_send()
        passed[i].wait_send()


def sum_kernel(
    part_ref, rest_ref, gain_ref, out_ref, after_ref,
    got_far, got_own, forward, got_side, sems,
):
    me, near, far, across = partners()
    own_rows = rest_ref.shape[0]
    size = own_rows // PIECES

    def rows(chunk, i):
        return pl.ds(pl.multiple_of(chunk * own_rows + i * size, size), size)

    greet(near, far)
    first, second, third, fourth, fifth, sixth = [], [], [], [], [], []
    for i in range(PIECES):
        here = pl.ds(i * size, size)
        first.append(send(part_ref.at[rows(across, i)], got_far.at[here], sems.at[0], i, near))
        first[i].start()
    for i in range(PIECES):
        here = pl.ds(i * size, size)
        second.append(send(part_ref.at[rows(near, i)], got_own.at[here], sems.at[1], i, near))
        second[i].start()
    for i in range(PIECES):
        here = pl.ds(i * size, size)
        first[i].wait_recv()
        forward[here] = (
            part_ref[rows(far, i)].astype(jnp.float32) + got_far[here].astype(jnp.float32)
        ).astype(jnp.bfloat16)
        third.append(send(forward.at[here], got_side.at[here], sems.at[2], i, far))
        third[i].start()
    for i in range(PIECES):
        here = pl.ds(i * size, size)
        second[i].wait_recv()
        third[i].wait_recv()
        total = rest_ref[here] + (
            part_ref[rows(me, i)].astype(jnp.float32)
            + got_own[here].astype(jnp.float32)
            + got_side[here].astype(jnp.float32)
        )
        after_ref[here] = total
        out_ref[rows(me, i)] = norm_rows(total, gain_ref[...]).astype(jnp.bfloat16)
        fourth.append(send(out_ref.at[rows(me, i)], out_ref.at[rows(me, i)], sems.at[3], i, far))
        fourth[i].start()
        fifth.append(send(out_ref.at[rows(me, i)], out_ref.at[rows(me, i)], sems.at[4], i, near))
        fifth[i].start()
    for i in range(PIECES):
        fourth[i].wait_recv()
        sixth.append(send(out_ref.at[rows(far, i)], out_ref.at[rows(far, i)], sems.at[5], i, near))
        sixth[i].start()
    for i in range(PIECES):
        fifth[i].wait_recv()
        sixth[i].wait_recv()
    for i in range(PIECES):
        for copies in (first, second, third, fourth, fifth, sixth):
            copies[i].wait_send()


def sum_merge_kernel(
    part_ref, rest_ref, gain_ref, weight_ref, merged_ref,
    out_ref, weight, got_far, got_own, forward, got_side, sems, weight_sem,
):
    me, near, far, across = partners()
    own_rows = rest_ref.shape[0]
    size = own_rows // PIECES

    def rows(chunk, i):
        return pl.ds(pl.multiple_of(chunk * own_rows + i * size, size), size)

    fetch = pltpu.make_async_copy(weight_ref, weight, weight_sem)
    fetch.start()
    greet(near, far)
    first, second, third, fourth, fifth, sixth = [], [], [], [], [], []
    for i in range(PIECES):
        here = pl.ds(i * size, size)
        first.append(send(part_ref.at[rows(across, i)], got_far.at[here], sems.at[0], i, near))
        first[i].start()
    for i in range(PIECES):
        here = pl.ds(i * size, size)
        second.append(send(part_ref.at[rows(near, i)], got_own.at[here], sems.at[1], i, near))
        second[i].start()
    for i in range(PIECES):
        here = pl.ds(i * size, size)
        first[i].wait_recv()
        forward[here] = (
            part_ref[rows(far, i)].astype(jnp.float32) + got_far[here].astype(jnp.float32)
        ).astype(jnp.bfloat16)
        third.append(send(forward.at[here], got_side.at[here], sems.at[2], i, far))
        third[i].start()
    for i in range(PIECES):
        here = pl.ds(i * size, size)
        second[i].wait_recv()
        third[i].wait_recv()
        total = rest_ref[here] + (
            part_ref[rows(me, i)].astype(jnp.float32)
            + got_own[here].astype(jnp.float32)
            + got_side[here].astype(jnp.float32)
        )
        out_ref[rows(me, i)] = norm_rows(total, gain_ref[...]).astype(jnp.bfloat16)
        fourth.append(send(out_ref.at[rows(me, i)], out_ref.at[rows(me, i)], sems.at[3], i, far))
        fourth[i].start()
        fifth.append(send(out_ref.at[rows(me, i)], out_ref.at[rows(me, i)], sems.at[4], i, near))
        fifth[i].start()
    full = out_ref.shape[1]

    def term(chunk):
        return lax.dot_general(
            out_ref[pl.ds(pl.multiple_of(chunk * own_rows, own_rows), own_rows)],
            weight[:, pl.ds(pl.multiple_of(chunk * full, 128), full)],
            (((1,), (1,)), ((), ())),
            preferred_element_type=jnp.float32,
        )

    fetch.wait()
    merged = term(me)
    for i in range(PIECES):
        fourth[i].wait_recv()
        sixth.append(send(out_ref.at[rows(far, i)], out_ref.at[rows(far, i)], sems.at[5], i, near))
        sixth[i].start()
    merged = merged + term(far)
    for i in range(PIECES):
        fifth[i].wait_recv()
    merged = merged + term(near)
    for i in range(PIECES):
        sixth[i].wait_recv()
    merged_ref[...] = (merged + term(across)).astype(jnp.bfloat16)
    for i in range(PIECES):
        for copies in (first, second, third, fourth, fifth, sixth):
            copies[i].wait_send()


def mlp_kernel(x_ref, up_ref, down_ref, out_ref, lifted, total):
    step = pl.program_id(0)
    last = pl.num_programs(0) - 1

    def lift():
        return jnp.dot(x_ref[...], up_ref[...], preferred_element_type=jnp.float32)

    def lower(values):
        hidden = 0.5 * values * (1.0 + lax.erf(values * (0.5**0.5)))
        return jnp.dot(
            hidden.astype(jnp.bfloat16), down_ref[...], preferred_element_type=jnp.float32
        )

    @pl.when(step == 0)
    def _():
        total[...] = jnp.zeros_like(total)
        lifted[...] = lift()

    @pl.when((step > 0) & (step < last))
    def _():
        values = lifted[...]
        later = lift()
        total[...] += lower(values)
        lifted[...] = later

    @pl.when(step == last)
    def _():
        out_ref[...] = (total[...] + lower(lifted[...])).astype(jnp.bfloat16)


def route_kernel(sent_ref, hot_ref, pick_ref, out_ref, first, second, third, sems):
    count = lax.axis_size("blk")
    me = lax.axis_index("blk")
    others = [lax.rem(me + step, count) for step in range(1, count)]
    barrier = pltpu.get_barrier_semaphore()
    for other in others:
        pl.semaphore_signal(barrier, inc=1, device_id={"blk": other}, device_id_type=MESH)
    pl.semaphore_wait(barrier, count - 1)

    def hop(source, target, number):
        size = source.shape[0] // count

        def rows(index):
            return pl.ds(pl.multiple_of(index * size, size), size)

        copies = []
        for step, other in enumerate(others):
            copies.append(
                pltpu.make_async_remote_copy(
                    src_ref=source.at[rows(other)],
                    dst_ref=target.at[rows(me)],
                    send_sem=sems.at[number, 0, step],
                    recv_sem=sems.at[number, 1, step],
                    device_id={"blk": other},
                    device_id_type=MESH,
                )
            )
            copies[step].start()
        target[rows(me)] = source[rows(me)]
        for copy in copies:
            copy.wait_recv()
        return copies

    one = hop(sent_ref, first, 0)
    second[...] = jnp.dot(
        hot_ref[...], first[...], preferred_element_type=jnp.float32
    ).astype(jnp.bfloat16)
    two = hop(second, third, 1)
    out_ref[...] = jnp.dot(
        pick_ref[...], third[...], preferred_element_type=jnp.float32
    ).astype(jnp.bfloat16)
    for copy in one + two:
        copy.wait_send()


def vmem(count):
    return [pl.BlockSpec(memory_space=pltpu.VMEM)] * count


def gather_norm(x, gain, collective_id):
    rows, width = x.shape
    full = width * TP
    pair = pltpu.SemaphoreType.DMA((2, PIECES))
    return pl.pallas_call(
        gather_kernel,
        out_shape=(
            jax.ShapeDtypeStruct((rows, full), jnp.bfloat16),
            jax.ShapeDtypeStruct((rows // TP, full), jnp.float32),
        ),
        in_specs=vmem(2),
        out_specs=tuple(vmem(2)),
        scratch_shapes=[
            pltpu.VMEM((TP, rows, width), jnp.bfloat16),
            pair, pair, pair, pltpu.SemaphoreType.DMA,
        ],
        compiler_params=pltpu.CompilerParams(
            collective_id=collective_id, has_side_effects=True, vmem_limit_bytes=40 * 2**20
        ),
        name="gather_norm",
    )(x, gain.reshape(1, -1))


def sum_norm(part, rest, gain, collective_id):
    rows, full = part.shape
    own = (rows // TP, full)
    return pl.pallas_call(
        sum_kernel,
        out_shape=(
            jax.ShapeDtypeStruct((rows, full), jnp.bfloat16),
            jax.ShapeDtypeStruct(own, jnp.float32),
        ),
        in_specs=vmem(3),
        out_specs=tuple(vmem(2)),
        scratch_shapes=[pltpu.VMEM(own, jnp.bfloat16)] * 4
        + [pltpu.SemaphoreType.DMA((6, 2, PIECES))],
        compiler_params=pltpu.CompilerParams(
            collective_id=collective_id, has_side_effects=True, vmem_limit_bytes=40 * 2**20
        ),
        name="sum_norm",
    )(part, rest, gain.reshape(1, -1))


def sum_merge(part, rest, gain, weight, collective_id):
    rows, full = part.shape
    own = (rows // TP, full)
    return pl.pallas_call(
        sum_merge_kernel,
        out_shape=jax.ShapeDtypeStruct((rows // TP, weight.shape[0]), jnp.bfloat16),
        in_specs=vmem(3) + [pl.BlockSpec(memory_space=pl.ANY)],
        out_specs=vmem(1)[0],
        scratch_shapes=[
            pltpu.VMEM(part.shape, jnp.bfloat16),
            pltpu.VMEM(weight.shape, jnp.bfloat16),
        ]
        + [pltpu.VMEM(own, jnp.bfloat16)] * 4
        + [pltpu.SemaphoreType.DMA((6, 2, PIECES)), pltpu.SemaphoreType.DMA],
        compiler_params=pltpu.CompilerParams(
            collective_id=collective_id, has_side_effects=True, vmem_limit_bytes=40 * 2**20
        ),
        name="sum_merge",
    )(part, rest, gain.reshape(1, -1), weight)


def mlp(x, up, down):
    rows, full = x.shape
    tile = 512
    steps = up.shape[1] // tile
    return pl.pallas_call(
        mlp_kernel,
        grid=(steps + 1,),
        out_shape=jax.ShapeDtypeStruct((rows, full), jnp.bfloat16),
        in_specs=[
            pl.BlockSpec((rows, full), lambda i: (0, 0)),
            pl.BlockSpec((full, tile), lambda i: (0, jnp.minimum(i, steps - 1))),
            pl.BlockSpec((tile, full), lambda i: (jnp.maximum(i - 1, 0), 0)),
        ],
        out_specs=pl.BlockSpec((rows, full), lambda i: (0, 0)),
        scratch_shapes=[
            pltpu.VMEM((rows, tile), jnp.float32),
            pltpu.VMEM((rows, full), jnp.float32),
        ],
        compiler_params=pltpu.CompilerParams(vmem_limit_bytes=40 * 2**20),
        name="mlp",
    )(x, up, down)


def route_rows(sent, hot, pick, collective_id):
    count = lax.axis_size("blk")
    wide = (hot.shape[0], sent.shape[1])
    return pl.pallas_call(
        route_kernel,
        out_shape=jax.ShapeDtypeStruct(sent.shape, jnp.bfloat16),
        in_specs=vmem(3),
        out_specs=vmem(1)[0],
        scratch_shapes=[
            pltpu.VMEM(sent.shape, jnp.bfloat16),
            pltpu.VMEM(wide, jnp.bfloat16),
            pltpu.VMEM(wide, jnp.bfloat16),
            pltpu.SemaphoreType.DMA((2, 2, count - 1)),
        ],
        compiler_params=pltpu.CompilerParams(
            collective_id=collective_id, has_side_effects=True, vmem_limit_bytes=40 * 2**20
        ),
        name="route_rows",
    )(sent, hot, pick)


def route(tokens, block_split, req_lengths, req_owners):
    count = lax.axis_size("blk")
    rows, width = tokens.shape
    groups = rows // 4
    block_groups = groups // 2
    each = groups // count
    requests = req_lengths.shape[0]
    room = (groups + (requests // count) * (count - 1)) // count
    room = (room + 3) // 4 * 4
    index = lax.axis_index("blk")
    position = jnp.arange(requests, dtype=jnp.int32)
    ends = jnp.sum(
        jnp.where(position[None, :] <= position[:, None], req_lengths[None, :], 0), axis=1
    )
    starts = ends - req_lengths
    earlier = (req_owners[None, :] == req_owners[:, None]) & (position[None, :] < position[:, None])
    offset = jnp.sum(jnp.where(earlier, req_lengths[None, :], 0), axis=1)
    spot = jnp.arange(groups, dtype=jnp.int32)
    local = (spot % each) * count + index
    place = (spot // each) * 2 + local // block_groups
    places = jnp.arange(block_split.shape[0], dtype=jnp.int32)
    block = jnp.sum(jnp.where(place[:, None] == places[None, :], block_split[None, :], 0), axis=1)
    packed = block * block_groups + local % block_groups
    inside = (starts[None, :] <= packed[:, None]) & (packed[:, None] < ends[None, :])
    goal = jnp.sum(
        jnp.where(inside, (req_owners * groups + offset - starts)[None, :], 0), axis=1
    ) + packed
    owner = goal // groups
    rank = jnp.sum(
        ((owner[None, :] == owner[:, None]) & (goal[None, :] < goal[:, None])).astype(jnp.int32),
        axis=1,
    )
    out_spot = owner * room + rank
    chosen = (
        (req_owners[None, :] == index)
        & (offset[None, :] <= spot[:, None])
        & (spot[:, None] < (offset + req_lengths)[None, :])
    )
    wanted = jnp.sum(jnp.where(chosen, (starts - offset)[None, :], 0), axis=1) + spot
    request = jnp.sum(jnp.where(chosen, position[None, :], 0), axis=1)
    via = wanted % count
    turn = jnp.sum(
        ((via[None, :] == via[:, None]) & (spot[None, :] < spot[:, None])).astype(jnp.int32), axis=1
    )
    in_spot = via * room + turn

    def pick(hot, array):
        return jnp.dot(
            hot.astype(jnp.bfloat16), array, preferred_element_type=jnp.float32
        ).astype(jnp.bfloat16)

    row = jnp.arange(rows, dtype=jnp.int32)
    via_row = row // (4 * each)
    q_row = row // 4 % each
    source = (q_row * count + via_row) * 4 + row % 4
    sent = pick(source[:, None] == row[None, :], tokens)
    row_goal = jnp.repeat(out_spot, 4) * 4 + row % 4
    slots = jnp.arange(count * room * 4, dtype=jnp.int32)
    hot = (slots[:, None] == row_goal[None, :]).astype(jnp.bfloat16)
    row_from = jnp.tile(in_spot, 4) * 4 + row // groups
    chosen_rows = (row_from[:, None] == slots[None, :]).astype(jnp.bfloat16)
    return route_rows(sent, hot, chosen_rows, 4), request


def body(
    tokens,
    block_split,
    req_lengths,
    req_owners,
    norm1_gain,
    qkv_weight,
    out_weight,
    norm2_gain,
    up_weight,
    down_weight,
    merge_gain,
    merge_weight,
):
    rows, width = tokens.shape
    routed, request = route(tokens, block_split, req_lengths, req_owners)
    normed1, rest = gather_norm(routed, norm1_gain, 1)
    projected = jnp.einsum(
        "td,dcf->ctf", normed1, qkv_weight, preferred_element_type=jnp.float32
    ).astype(jnp.bfloat16)
    heads = width // HDIM
    queries, keys, values = (projected[c].reshape(rows, heads, HDIM) for c in range(3))
    segment = jnp.tile(request, 4)
    same = (segment[:, None] == segment[None, :])[None, :, :]
    scores = jnp.einsum(
        "qhd,khd->hqk", queries, keys, preferred_element_type=jnp.float32
    ) * HDIM ** (-0.5)
    scores = jnp.where(same, scores, MASKED)
    weights = jnp.exp(scores - jnp.max(scores, axis=2, keepdims=True))
    totals = jnp.sum(weights, axis=2)
    mixed = jnp.einsum(
        "hqk,khd->qhd", weights.astype(jnp.bfloat16), values, preferred_element_type=jnp.float32
    )
    attended = (mixed / jnp.transpose(totals)[:, :, None]).reshape(rows, width).astype(jnp.bfloat16)
    part = jnp.dot(attended, out_weight, preferred_element_type=jnp.float32).astype(jnp.bfloat16)
    normed2, rest = sum_norm(part, rest, norm2_gain, 2)
    part = mlp(normed2, up_weight, down_weight)
    return sum_merge(part, rest, merge_gain, merge_weight.T, 3)


def solution(mesh):
    return jax.shard_map(
        body,
        mesh=mesh,
        in_specs=(
            P("blk", "tp"),
            P(),
            P(),
            P(),
            P(),
            P(None, None, "tp"),
            P("tp", None),
            P(),
            P(None, "tp"),
            P("tp", None),
            P(),
            P(None, "tp"),
        ),
        out_specs=P("blk", "tp"),
        check_vma=False,
    )
```
